32 devices in a mesh: fsdp: 8 (over y, x, core), tp: 4 (over z).
Axes of the slice: x: 2, y: 2, z: 4, core: 2. Of those that a mesh axis runs over, the one named last changes fastest.
Arguments:
- inputs: bfloat16 [8192, 768], P(('fsdp', 'tp')), may hold values from -6 to 6
- cotangent: bfloat16 [8192, 768], P(('fsdp', 'tp')), may hold values from -6 to 6
- qkv_weight: bfloat16 [2, 3, 768, 768], P(None, None, 'fsdp', 'tp'), may hold values from -0.21875 to 0.21875
- out_weight: bfloat16 [2, 768, 768], P(None, 'tp', 'fsdp'), may hold values from -0.875 to 0.875
- attn_gain: bfloat16 [2, 768], P(None, 'fsdp'), may hold values from 0.25 to 1.75
- ffn_gain: bfloat16 [2, 768], P(None, 'fsdp'), may hold values from 0.25 to 1.75
- router_weight: bfloat16 [2, 768, 4], P(None, 'fsdp'), may hold values from -0.15625 to 0.15625
- in_weight: bfloat16 [2, 4, 768, 3072], P(None, None, 'fsdp', 'tp'), may hold values from -0.21875 to 0.21875
- down_weight: bfloat16 [2, 4, 3072, 768], P(None, None, 'tp', 'fsdp'), may hold values from -0.4375 to 0.4375
- routes: int32 [8192], P('fsdp'), may hold values from 0 to 3, as said below
- slots: int32 [8192], P('fsdp'), may hold values from 0 to 256, as said below
Outputs:
- outputs: float32 [8192, 768], P(('fsdp', 'tp'))
- d_inputs: float32 [8192, 768], P(('fsdp', 'tp'))
- d_qkv_weight: float32 [2, 3, 768, 768], P(None, None, 'fsdp', 'tp')
- d_out_weight: float32 [2, 768, 768], P(None, 'tp', 'fsdp')
- d_attn_gain: float32 [2, 768], P(None, 'fsdp')
- d_ffn_gain: float32 [2, 768], P(None, 'fsdp')
- d_router_weight: float32 [2, 768, 4], P(None, 'fsdp')
- d_in_weight: float32 [2, 4, 768, 3072], P(None, None, 'fsdp', 'tp')
- d_down_weight: float32 [2, 4, 3072, 768], P(None, None, 'tp', 'fsdp')
The draws below stay inside these ranges and needn't reach their ends.
Inputs may be any that keep to these rules, and one draw needn't show every extreme that they name: `routes`: the expert of a token; in each group one expert drawn from the seed is named by more than 256 tokens. A token's rank, in order of position, among the tokens of its group with the same route, with ranks of 256 or more given as 256 (the token is dropped); in every group some expert fills all 256 slots and drops tokens.
All inputs are finite; a program needn't handle non-finite values.
Results may differ from the reference program's by a relative error of at most 0.028.
Values may be sent and summed in bfloat16 or wider, within the bound.
A program may use at most 192 MiB of HBM per device.

```python
import jax
import jax.numpy as jnp
from jax import lax

D = 768
H = 12
DH = 64
FF = 3072
E = 4
LAYERS = 2
SEQ = 1024
SEQS = 1
CAP = 256
TOKENS = 8192


def route_table(key):
    group_tok = SEQS * SEQ
    groups = TOKENS // group_tok
    first, second, third = jax.random.split(key, 3)
    hot_expert = jax.random.randint(first, (groups, 1), 0, E)
    spread_route = jax.random.randint(second, (groups, group_tok), 0, E)
    order = jax.vmap(lambda sub_key: jax.random.permutation(sub_key, group_tok))(jax.random.split(third, groups))
    forced = order < CAP + CAP // 4
    route = jnp.where(forced, hot_expert, spread_route).astype(jnp.int32)
    one_hot = (route[:, :, None] == jnp.arange(E, dtype=jnp.int32)[None, None, :]).astype(jnp.int32)
    ranks = jnp.sum((jnp.cumsum(one_hot, axis=1) - 1) * one_hot, -1)
    slot = jnp.minimum(ranks, CAP).astype(jnp.int32)
    return (route.reshape(-1), slot.reshape(-1))


def draw_routes(key, part):
    return route_table(key)[0]


def draw_slots(key, part):
    return route_table(key)[1]


def block_scale(key, shape, cuts, smallest, largest):
    def one(dim, blocks):
        steps = jax.random.uniform(jax.random.fold_in(jax.random.fold_in(key, 6), dim), (blocks,), jnp.float32, smallest / len(cuts), largest / len(cuts))
        return jnp.repeat(jnp.exp(steps), shape[dim] // blocks).reshape((-1,) + (1,) * (len(shape) - dim - 1))

    loudness = one(*cuts[0])
    for cut in cuts[1:]:
        loudness = loudness * one(*cut)
    return loudness


def centred(own_key, dims, scale, limit, cuts=(), held_as=jnp.bfloat16):
    values = jax.random.normal(own_key, dims, jnp.float32) * scale
    if len(cuts) > 0:
        values = block_scale(own_key, dims, cuts, -0.22, 0.18) * values
    return jnp.clip(values, min=-limit, max=limit).astype(held_as)


def setup_inputs(seed: int = 0) -> dict:
    key_of = jax.random.split(jax.random.key(seed), 12)
    inputs = centred(key_of[0], (TOKENS, D), 1.0, 6.0, ((0, 32),))
    cotangent = centred(key_of[1], (TOKENS, D), 1.0, 6.0, ((0, 32),))
    qkv_weight = centred(key_of[2], (LAYERS, 3, D, H * DH), D ** -0.5, 0.21875, ((2, 8), (3, 4)))
    out_weight = centred(key_of[3], (LAYERS, H * DH, D), (H * DH // 16) ** -0.5, 0.875, ((1, 4), (2, 8)))
    attn_gain = jnp.clip(1.0 + 0.15 * jax.random.normal(key_of[4], (LAYERS, D), jnp.float32), 0.25, 1.75).astype(jnp.bfloat16)
    ffn_gain = jnp.clip(1.0 + 0.15 * jax.random.normal(key_of[5], (LAYERS, D), jnp.float32), 0.25, 1.75).astype(jnp.bfloat16)
    router_weight = centred(key_of[6], (LAYERS, D, E), (2 * D) ** -0.5, 0.15625, ((1, 8),))
    in_weight = centred(key_of[7], (LAYERS, E, D, FF), D ** -0.5, 0.21875, ((2, 8), (3, 4)))
    down_weight = centred(key_of[8], (LAYERS, E, FF, D), (FF // 16) ** -0.5, 0.4375, ((2, 4), (3, 8)))
    routes = draw_routes(jax.random.fold_in(key_of[11], 71), 0)
    slots = draw_slots(jax.random.fold_in(key_of[11], 71), 0)
    return dict(inputs=inputs, cotangent=cotangent, qkv_weight=qkv_weight, out_weight=out_weight, attn_gain=attn_gain, ffn_gain=ffn_gain, router_weight=router_weight, in_weight=in_weight, down_weight=down_weight, routes=routes, slots=slots)


EPSILON = 1e-06
HIGH = lax.Precision.HIGHEST

@jax.custom_vjp
def low(v):
    return lax.optimization_barrier(v.astype(jnp.bfloat16)).astype(jnp.float32)

@jax.custom_vjp
def low_back(v):
    return v

def low_keep(v):
    return (low(v), None)

def low_pass(kept, grad):
    return (grad,)

def back_keep(v):
    return (v, None)

def back_low(kept, grad):
    return (low(grad),)
low.defvjp(low_keep, low_pass)
low_back.defvjp(back_keep, back_low)

def normed(hidden, gain_row):
    scale_inv = lax.rsqrt(lax.optimization_barrier(jnp.mean(hidden * hidden, -1, keepdims=True)) + EPSILON)
    return hidden * scale_inv * gain_row

def slot_tables(route_part, slot_part, experts, capacity):
    is_live = slot_part < capacity
    position = jnp.where(is_live, route_part * capacity + slot_part, experts * capacity).astype(jnp.int32)
    row_total = route_part.shape[0]
    token_of = jnp.zeros((experts * capacity + 1,), jnp.int32).at[position].set(jnp.arange(row_total, dtype=jnp.int32))[:-1]
    filled = jnp.zeros((experts * capacity + 1,), jnp.bool_).at[position].set(True)[:-1]
    return (is_live, jnp.where(is_live, position, 0).astype(jnp.int32), token_of, filled)

def attend(triple):
    query, key_rows, value_rows = triple
    scores = low_back(jnp.einsum('qhd,khd->hqk', query, key_rows, precision=HIGH)) * DH ** (-0.5)
    probs = low(jax.nn.softmax(scores, -1))
    return jnp.einsum('hqk,khd->qhd', probs, value_rows, precision=HIGH)

def encoder_layer(hidden, layer_weights, route_part, slot_part):
    wqkv, wout, gain_one, gain_two, router_full, win, wdown = layer_weights
    group_tok = hidden.shape[0]
    a_rows = low(normed(hidden, gain_one))
    qkv = low(low_back(jnp.einsum('td,cdf->ctf', a_rows, wqkv, precision=HIGH)))
    shaped = qkv.reshape(3, SEQS, SEQ, H, DH)
    mixed = lax.map(jax.checkpoint(attend), (shaped[0], shaped[1], shaped[2]))
    mixed = low(low_back(mixed)).reshape(group_tok, H * DH)
    attn = low_back(jnp.dot(mixed, wout, precision=HIGH))
    middle = hidden + attn
    b_rows = low(normed(middle, gain_two))
    logits = jnp.dot(b_rows, router_full, precision=HIGH)
    probs = jax.nn.softmax(logits, -1)
    gate = jnp.take_along_axis(probs, route_part[:, None], -1)[:, 0]
    is_live, position, token_of, filled = slot_tables(route_part, slot_part, E, CAP)
    buffer = jnp.where(filled[:, None], b_rows[token_of], 0.0).reshape(E, CAP, D)
    pre = low_back(jnp.einsum('ecd,edf->ecf', buffer, win, precision=HIGH))
    act = low(jax.nn.gelu(pre))
    expert_out = jnp.einsum('ecf,efd->ecd', act, wdown, precision=HIGH).reshape(E * CAP, D)
    combined = low_back(jnp.where(is_live[:, None], expert_out[position], 0.0))
    return middle + gate[:, None] * combined

def encoder(rows, weight_set, route_part, slot_part):
    hidden = rows
    for layer_index in range(LAYERS):
        layer_weights = tuple((weight_array[layer_index] for weight_array in weight_set))
        hidden = encoder_layer(hidden, layer_weights, route_part, slot_part)
    return hidden

def reference(inputs, cotangent, qkv_weight, out_weight, attn_gain, ffn_gain, router_weight, in_weight, down_weight, routes, slots):
    params = tuple((weight_array.astype(jnp.float32) for weight_array in (qkv_weight, out_weight, attn_gain, ffn_gain, router_weight, in_weight, down_weight)))
    group_tok = SEQS * SEQ
    groups = TOKENS // group_tok
    rows_all = inputs.astype(jnp.float32).reshape(groups, group_tok, D)
    upstream_all = cotangent.astype(jnp.float32).reshape(groups, group_tok, D)
    route_all = routes.reshape(groups, group_tok)
    slot_all = slots.reshape(groups, group_tok)

    def one_group(totals, item):
        rows, upstream, route_part, slot_part = item

        def forward(rows_in, weight_set):
            return encoder(rows_in, weight_set, route_part, slot_part)
        result, pull_back = jax.vjp(forward, rows, params)
        d_rows, d_weights = pull_back(upstream)
        return (jax.tree.map(jnp.add, totals, d_weights), (result, d_rows))
    zeros = jax.tree.map(jnp.zeros_like, params)
    totals, (results, d_rows) = lax.scan(one_group, zeros, (rows_all, upstream_all, route_all, slot_all))
    return (results.reshape(TOKENS, D), d_rows.reshape(TOKENS, D), totals[0], totals[1], totals[2], totals[3], totals[4], totals[5], totals[6])
```

```python
import jax
import jax.numpy as jnp
from jax import lax
from jax.experimental import pallas as pl
from jax.experimental.pallas import tpu as pltpu
from jax.sharding import PartitionSpec as P

DH = 64
LAYERS = 2
BLOCK = 256

EPSILON = 1e-06
HIGH = lax.Precision.HIGHEST
BF = jnp.bfloat16
F32 = jnp.float32
GELU_C = 0.7978845608028654
GELU_A = 0.044715
VMEM_BYTES = 48 * 1024 * 1024


def dot(left, right, left_dim, right_dim):
    return lax.dot_general(
        left, right, (((left_dim,), (right_dim,)), ((), ())), preferred_element_type=F32
    )


def normed(hidden, gain_row):
    scale_inv = lax.rsqrt(jnp.mean(hidden * hidden, -1, keepdims=True) + EPSILON)
    return hidden * scale_inv * gain_row


def normed_back(hidden, gain_row, upstream):
    _, pull_back = jax.vjp(normed, hidden, gain_row)
    return pull_back(upstream)


def params():
    return pltpu.CompilerParams(
        dimension_semantics=("arbitrary",), vmem_limit_bytes=VMEM_BYTES
    )


def whole_spec(array):
    rank = len(array.shape)
    return pl.BlockSpec(array.shape, lambda i: (0,) * rank)


def attend_ahead_body(a_ref, w_ref, part_ref, qkv_ref, mixed_ref):
    step = pl.program_id(0)
    heads_dim = mixed_ref.shape[1]
    heads = heads_dim // DH

    @pl.when(step == 0)
    def _():
        qkv_ref[...] = dot(a_ref[...], w_ref[:, : 3 * heads_dim], 1, 0).astype(BF)

    rows = pl.ds(pl.multiple_of(step * BLOCK, BLOCK), BLOCK)
    parts = []
    for head in range(heads):
        low = head * DH
        query = qkv_ref[rows, low : low + DH] * BF(DH**-0.5)
        key_rows = qkv_ref[:, heads_dim + low : heads_dim + low + DH]
        value_rows = qkv_ref[:, 2 * heads_dim + low : 2 * heads_dim + low + DH]
        scores = dot(query, key_rows, 1, 1)
        expon = jnp.exp(scores - jnp.max(scores, -1, keepdims=True))
        total = jnp.sum(expon, -1, keepdims=True)
        probs = (expon * (1.0 / total)).astype(BF)
        parts.append(dot(probs, value_rows, 1, 0))
    mixed = jnp.concatenate(parts, -1).astype(BF)
    mixed_ref[...] = mixed
    part_ref[...] = dot(mixed, w_ref[:, 3 * heads_dim : 4 * heads_dim], 1, 1).astype(BF)


def attend_ahead(a_rows, w_pack, heads_dim):
    tokens, width = a_rows.shape
    return pl.pallas_call(
        attend_ahead_body,
        grid=(tokens // BLOCK,),
        in_specs=[whole_spec(a_rows), whole_spec(w_pack)],
        out_specs=[
            pl.BlockSpec((BLOCK, width), lambda i: (i, 0)),
            pl.BlockSpec((tokens, 3 * heads_dim), lambda i: (0, 0)),
            pl.BlockSpec((BLOCK, heads_dim), lambda i: (i, 0)),
        ],
        out_shape=[
            jax.ShapeDtypeStruct((tokens, width), BF),
            jax.ShapeDtypeStruct((tokens, 3 * heads_dim), BF),
            jax.ShapeDtypeStruct((tokens, heads_dim), BF),
        ],
        compiler_params=params(),
        cost_estimate=pl.CostEstimate(
            flops=2 * tokens * heads_dim * (4 * width + 4 * 2 * tokens),
            bytes_accessed=8 * 1024 * 1024,
            transcendentals=tokens * tokens * heads_dim // DH,
        ),
    )(a_rows, w_pack)


def attend_behind_body(
    da_ref, a_ref, qkv_ref, mixed_ref, w_ref, back_ref, grad_ref, dqkv_ref, acc_ref
):
    step = pl.program_id(0)
    heads_dim = mixed_ref.shape[1]
    heads = heads_dim // DH

    @pl.when(step == 0)
    def _():
        acc_ref[...] = jnp.zeros_like(acc_ref)

    rows = pl.ds(pl.multiple_of(step * BLOCK, BLOCK), BLOCK)
    d_mixed = dot(da_ref[rows, :], w_ref[:, 3 * heads_dim : 4 * heads_dim], 1, 0).astype(BF)
    query_parts = []
    key_parts = []
    value_parts = []
    for head in range(heads):
        low = head * DH
        query = qkv_ref[rows, low : low + DH]
        key_rows = qkv_ref[:, heads_dim + low : heads_dim + low + DH]
        value_rows = qkv_ref[:, 2 * heads_dim + low : 2 * heads_dim + low + DH]
        d_mixed_one = d_mixed[:, low : low + DH]
        scores = dot(key_rows, query * BF(DH**-0.5), 1, 1)
        expon = jnp.exp(scores - jnp.max(scores, 0, keepdims=True))
        probs = expon * (1.0 / jnp.sum(expon, 0, keepdims=True))
        d_probs = dot(value_rows, d_mixed_one, 1, 1)
        weighted = probs * d_probs
        d_scores = weighted - probs * jnp.sum(weighted, 0, keepdims=True)
        d_scaled = (d_scores * (DH**-0.5)).astype(BF)
        query_parts.append(dot(d_scaled, key_rows, 0, 0))
        key_parts.append(dot(d_scaled, query, 1, 0))
        value_parts.append(dot(probs.astype(BF), d_mixed_one, 1, 0))
    dqkv_ref[rows, :heads_dim] = jnp.concatenate(query_parts, -1).astype(BF)
    acc_ref[...] += jnp.concatenate(key_parts + value_parts, -1)

    @pl.when(step == pl.num_programs(0) - 1)
    def _():
        dqkv_ref[:, heads_dim:] = acc_ref[...].astype(BF)
        back_ref[...] = dot(dqkv_ref[...], w_ref[:, : 3 * heads_dim], 1, 1).astype(BF)
        grad_ref[:, : 3 * heads_dim] = dot(a_ref[...], dqkv_ref[...], 0, 0).astype(BF)
        grad_ref[:, 3 * heads_dim :] = dot(da_ref[...], mixed_ref[...], 0, 0).astype(BF)


def attend_behind(da_rows, a_rows, qkv, mixed, w_pack):
    tokens, width = a_rows.shape
    heads_dim = mixed.shape[1]
    operands = (da_rows, a_rows, qkv, mixed, w_pack)
    return pl.pallas_call(
        attend_behind_body,
        grid=(tokens // BLOCK,),
        in_specs=[whole_spec(operand) for operand in operands],
        out_specs=[
            pl.BlockSpec((tokens, width), lambda i: (0, 0)),
            pl.BlockSpec((width, 4 * heads_dim), lambda i: (0, 0)),
        ],
        out_shape=[
            jax.ShapeDtypeStruct((tokens, width), BF),
            jax.ShapeDtypeStruct((width, 4 * heads_dim), BF),
        ],
        scratch_shapes=[
            pltpu.VMEM((tokens, 3 * heads_dim), BF),
            pltpu.VMEM((tokens, 2 * heads_dim), F32),
        ],
        compiler_params=params(),
        cost_estimate=pl.CostEstimate(
            flops=2 * tokens * heads_dim * (8 * width + 4 * 5 * tokens),
            bytes_accessed=10 * 1024 * 1024,
            transcendentals=tokens * tokens * heads_dim // DH,
        ),
    )(*operands)


def pick_rows(position_ref, step, capacity):
    tokens = position_ref.shape[1]
    slot = lax.broadcasted_iota(jnp.int32, (capacity, tokens), 0) + step * capacity
    return jnp.where(slot == position_ref[...], 1.0, 0.0).astype(BF)


def place_rows(position_ref, slots_total):
    tokens = position_ref.shape[0]
    slot = lax.broadcasted_iota(jnp.int32, (tokens, slots_total), 1)
    return jnp.where(slot == position_ref[...], 1.0, 0.0).astype(BF)


def experts_ahead_body(b_ref, row_ref, col_ref, w_ref, out_ref, buffer_ref, pre_ref, eo_ref):
    step = pl.program_id(0)
    capacity, hidden = pre_ref.shape
    buffer = dot(pick_rows(row_ref, step, capacity), b_ref[...], 1, 0).astype(BF)
    buffer_ref[...] = buffer
    pre = dot(buffer, w_ref[:, :hidden], 1, 0)
    pre_ref[...] = pre
    act = (0.5 * pre * (1.0 + jnp.tanh(GELU_C * (pre + GELU_A * pre * pre * pre)))).astype(BF)
    rows = pl.ds(pl.multiple_of(step * capacity, capacity), capacity)
    eo_ref[rows, :] = dot(act, w_ref[:, hidden:], 1, 1).astype(BF)

    @pl.when(step == pl.num_programs(0) - 1)
    def _():
        place = place_rows(col_ref, eo_ref.shape[0])
        out_ref[...] = dot(place, eo_ref[...], 1, 0).astype(BF)


def experts_ahead(b_rows, pos_row, pos_col, w_pack, experts, capacity):
    tokens, width = b_rows.shape
    both = w_pack.shape[1] // experts
    hidden = both // 2
    slots_total = experts * capacity
    return pl.pallas_call(
        experts_ahead_body,
        grid=(experts,),
        in_specs=[
            whole_spec(b_rows),
            whole_spec(pos_row),
            whole_spec(pos_col),
            pl.BlockSpec((width, both), lambda i: (0, i)),
        ],
        out_specs=[
            pl.BlockSpec((tokens, width), lambda i: (0, 0)),
            pl.BlockSpec((capacity, width), lambda i: (i, 0)),
            pl.BlockSpec((capacity, hidden), lambda i: (i, 0)),
        ],
        out_shape=[
            jax.ShapeDtypeStruct((tokens, width), BF),
            jax.ShapeDtypeStruct((slots_total, width), BF),
            jax.ShapeDtypeStruct((slots_total, hidden), F32),
        ],
        scratch_shapes=[pltpu.VMEM((slots_total, width), BF)],
        compiler_params=params(),
        cost_estimate=pl.CostEstimate(
            flops=2 * slots_total * width * (2 * hidden + 2 * tokens),
            bytes_accessed=20 * 1024 * 1024,
            transcendentals=slots_total * hidden,
        ),
    )(b_rows, pos_row, pos_col, w_pack)


def experts_behind_body(
    dc_ref, row_ref, col_ref, buffer_ref, pre_ref, w_ref, back_ref, grad_ref, db_ref
):
    step = pl.program_id(0)
    capacity, hidden = pre_ref.shape
    d_out = dot(pick_rows(row_ref, step, capacity), dc_ref[...], 1, 0).astype(BF)
    pre = pre_ref[...]
    squared = pre * pre
    bent = jnp.tanh(GELU_C * (pre + GELU_A * squared * pre))
    half = 0.5 * (1.0 + bent)
    act = (pre * half).astype(BF)
    grad_ref[:, hidden:] = dot(d_out, act, 0, 0).astype(BF)
    slope = half + 0.5 * pre * (1.0 - bent * bent) * (GELU_C * (1.0 + 3.0 * GELU_A * squared))
    d_pre = (dot(d_out, w_ref[:, hidden:], 1, 0) * slope).astype(BF)
    grad_ref[:, :hidden] = dot(buffer_ref[...], d_pre, 0, 0).astype(BF)
    rows = pl.ds(pl.multiple_of(step * capacity, capacity), capacity)
    db_ref[rows, :] = dot(d_pre, w_ref[:, :hidden], 1, 1).astype(BF)

    @pl.when(step == pl.num_programs(0) - 1)
    def _():
        place = place_rows(col_ref, db_ref.shape[0])
        back_ref[...] = dot(place, db_ref[...], 1, 0).astype(BF)


def experts_behind(dc_rows, pos_row, pos_col, buffer, pre, w_pack, experts, capacity):
    tokens, width = dc_rows.shape
    both = w_pack.shape[1] // experts
    hidden = both // 2
    slots_total = experts * capacity
    return pl.pallas_call(
        experts_behind_body,
        grid=(experts,),
        in_specs=[
            whole_spec(dc_rows),
            whole_spec(pos_row),
            whole_spec(pos_col),
            pl.BlockSpec((capacity, width), lambda i: (i, 0)),
            pl.BlockSpec((capacity, hidden), lambda i: (i, 0)),
            pl.BlockSpec((width, both), lambda i: (0, i)),
        ],
        out_specs=[
            pl.BlockSpec((tokens, width), lambda i: (0, 0)),
            pl.BlockSpec((width, both), lambda i: (0, i)),
        ],
        out_shape=[
            jax.ShapeDtypeStruct((tokens, width), BF),
            jax.ShapeDtypeStruct((width, experts * both), BF),
        ],
        scratch_shapes=[pltpu.VMEM((slots_total, width), BF)],
        compiler_params=params(),
        cost_estimate=pl.CostEstimate(
            flops=2 * slots_total * width * (4 * hidden + 2 * tokens),
            bytes_accessed=30 * 1024 * 1024,
            transcendentals=slots_total * hidden,
        ),
    )(dc_rows, pos_row, pos_col, buffer, pre, w_pack)


def gather_tokens(part):
    return lax.all_gather(part, "tp", axis=0, tiled=True)


def scatter_tokens(whole):
    return lax.psum_scatter(whole, "tp", scatter_dimension=0, tiled=True).astype(F32)


def local(
    inputs,
    cotangent,
    qkv_weight,
    out_weight,
    attn_gain,
    ffn_gain,
    router_weight,
    in_weight,
    down_weight,
    routes,
    slots,
):
    tp_index = lax.axis_index("tp")
    fsdp_index = lax.axis_index("fsdp")
    tok_here, width = inputs.shape
    shard = in_weight.shape[2]
    experts = in_weight.shape[1]
    hidden_units = in_weight.shape[3]
    heads_dim = qkv_weight.shape[3]
    group_tok = routes.shape[0]
    capacity = group_tok // experts

    packs = []
    for layer_index in range(LAYERS):
        small = [
            jnp.transpose(qkv_weight[layer_index], (1, 0, 2)).reshape(shard, 3 * heads_dim),
            out_weight[layer_index].T,
            attn_gain[layer_index][:, None],
            ffn_gain[layer_index][:, None],
            router_weight[layer_index],
        ]
        columns = 4 * heads_dim + 2 + experts
        small.append(jnp.zeros((shard, -columns % 128), BF))
        large = jnp.stack(
            [in_weight[layer_index], jnp.transpose(down_weight[layer_index], (0, 2, 1))], 1
        )
        large = jnp.transpose(large, (2, 0, 1, 3)).reshape(shard, experts * 2 * hidden_units)
        packs.append(
            (
                lax.all_gather(jnp.concatenate(small, 1), "fsdp", axis=0, tiled=True),
                lax.all_gather(large, "fsdp", axis=0, tiled=True),
            )
        )

    position = jnp.where(slots < capacity, routes * capacity + slots, -1)
    pos_row, pos_col = position[None, :], position[:, None]
    route_here = lax.dynamic_slice_in_dim(routes, tp_index * tok_here, tok_here)
    pick = (route_here[:, None] == jnp.arange(experts, dtype=jnp.int32)[None, :]).astype(F32)
    hidden = inputs.astype(F32)
    saved = []
    for layer_index in range(LAYERS):
        w_attn, w_experts = packs[layer_index]
        rest = w_attn[:, 4 * heads_dim : 4 * heads_dim + 2 + experts]
        rest_rows = rest.astype(F32).T
        gain_one, gain_two, router_rows = rest_rows[0], rest_rows[1], rest_rows[2:]
        a_here = normed(hidden, gain_one).astype(BF)
        a_rows = gather_tokens(a_here)
        partial_attn, qkv, mixed = attend_ahead(a_rows, w_attn, heads_dim)
        middle = hidden + scatter_tokens(partial_attn)
        b_here = normed(middle, gain_two).astype(BF)
        b_rows = gather_tokens(b_here)
        logits = jnp.dot(b_here, rest[:, 2:], preferred_element_type=F32)
        probs = jax.nn.softmax(logits, -1)
        gate = jnp.sum(probs * pick, -1)
        token_out, buffer, pre = experts_ahead(
            b_rows, pos_row, pos_col, w_experts, experts, capacity
        )
        combined = scatter_tokens(token_out)
        saved.append(
            (gain_one, gain_two, router_rows, hidden, a_rows, qkv, mixed, middle)
            + (b_here, probs, gate, combined, buffer, pre)
        )
        hidden = middle + gate[:, None] * combined
    upstream = cotangent.astype(F32)
    layer_grads = [None] * LAYERS
    small_sums = [None] * LAYERS
    for layer_index in reversed(range(LAYERS)):
        w_attn, w_experts = packs[layer_index]
        (gain_one, gain_two, router_rows, before, a_rows, qkv, mixed, middle) = saved[layer_index][:8]
        (b_here, probs, gate, combined, buffer, pre) = saved[layer_index][8:]
        dc_rows = gather_tokens((gate[:, None] * upstream).astype(BF))
        d_gate = jnp.sum(upstream * combined, -1)
        d_tokens, grad_experts = experts_behind(
            dc_rows, pos_row, pos_col, buffer, pre, w_experts, experts, capacity
        )
        d_logits = d_gate[:, None] * gate[:, None] * (pick - probs)
        d_b_here = scatter_tokens(d_tokens)
        for expert in range(experts):
            d_b_here = d_b_here + d_logits[:, expert : expert + 1] * router_rows[expert][None, :]
        grad_router = lax.dot_general(
            d_logits, b_here.astype(F32), (((0,), (0,)), ((), ())), precision=HIGH
        )
        d_middle, grad_gain_two = normed_back(middle, gain_two, d_b_here)
        d_middle = d_middle + upstream
        da_rows = gather_tokens(d_middle.astype(BF))
        d_a_rows, grad_attn = attend_behind(da_rows, a_rows, qkv, mixed, w_attn)
        d_before, grad_gain_one = normed_back(before, gain_one, scatter_tokens(d_a_rows))
        upstream = d_before + d_middle
        layer_grads[layer_index] = (
            lax.psum_scatter(grad_attn, "fsdp", scatter_dimension=0, tiled=True),
            lax.psum_scatter(grad_experts, "fsdp", scatter_dimension=0, tiled=True),
        )
        small_sums[layer_index] = jnp.concatenate(
            [grad_gain_one[None], grad_gain_two[None], grad_router], 0
        )
    sums = lax.psum(jnp.concatenate(small_sums, 0), ("fsdp", "tp"))
    sums = lax.dynamic_slice_in_dim(sums, fsdp_index * shard, shard, 1)
    sums = sums.reshape(LAYERS, 2 + experts, shard)
    attn_grads = jnp.stack([grads[0] for grads in layer_grads]).astype(F32)
    expert_grads = jnp.stack([grads[1] for grads in layer_grads]).astype(F32)
    expert_grads = expert_grads.reshape(LAYERS, shard, experts, 2, hidden_units)
    qkv_grads = attn_grads[:, :, : 3 * heads_dim].reshape(LAYERS, shard, 3, heads_dim)
    return (
        hidden,
        upstream,
        jnp.transpose(qkv_grads, (0, 2, 1, 3)),
        jnp.transpose(attn_grads[:, :, 3 * heads_dim :], (0, 2, 1)),
        sums[:, 0],
        sums[:, 1],
        jnp.transpose(sums[:, 2:], (0, 2, 1)),
        jnp.transpose(expert_grads[:, :, :, 0], (0, 2, 1, 3)),
        jnp.transpose(expert_grads[:, :, :, 1], (0, 2, 3, 1)),
    )


def solution(mesh):
    return jax.shard_map(
        local,
        mesh=mesh,
        in_specs=(
            P(("fsdp", "tp"), None),
            P(("fsdp", "tp"), None),
            P(None, None, "fsdp", "tp"),
            P(None, "tp", "fsdp"),
            P(None, "fsdp"),
            P(None, "fsdp"),
            P(None, "fsdp", None),
            P(None, None, "fsdp", "tp"),
            P(None, None, "tp", "fsdp"),
            P("fsdp"),
            P("fsdp"),
        ),
        out_specs=(
            P(("fsdp", "tp"), None),
            P(("fsdp", "tp"), None),
            P(None, None, "fsdp", "tp"),
            P(None, "tp", "fsdp"),
            P(None, "fsdp"),
            P(None, "fsdp"),
            P(None, "fsdp", None),
            P(None, None, "fsdp", "tp"),
            P(None, None, "tp", "fsdp"),
        ),
        check_vma=False,
    )
```

```python
import functools

import jax
import jax.numpy as jnp
from jax import lax
from jax.experimental import pallas as pl
from jax.experimental.pallas import tpu as pltpu
from jax.sharding import PartitionSpec as P

DH = 64
LAYERS = 2
BLOCK = 256

EPSILON = 1e-06
HIGH = lax.Precision.HIGHEST
BF = jnp.bfloat16
F32 = jnp.float32
GELU_C = 0.7978845608028654
GELU_A = 0.044715
VMEM_BYTES = 48 * 1024 * 1024


def dot(left, right, left_dim, right_dim):
    return lax.dot_general(
        left, right, (((left_dim,), (right_dim,)), ((), ())), preferred_element_type=F32
    )


def normed(hidden, gain_row):
    scale_inv = lax.rsqrt(jnp.mean(hidden * hidden, -1, keepdims=True) + EPSILON)
    return hidden * scale_inv * gain_row


def normed_back(hidden, gain_row, upstream):
    _, pull_back = jax.vjp(normed, hidden, gain_row)
    return pull_back(upstream)


def params():
    return pltpu.CompilerParams(
        dimension_semantics=("arbitrary",), vmem_limit_bytes=VMEM_BYTES
    )


def whole_spec(array):
    rank = len(array.shape)
    return pl.BlockSpec(array.shape, lambda i: (0,) * rank)


def attend_ahead_body(a_ref, w_ref, part_ref, qkv_ref, mixed_ref):
    step = pl.program_id(0)
    heads_dim = mixed_ref.shape[1]
    heads = heads_dim // DH

    @pl.when(step == 0)
    def _():
        qkv_ref[...] = dot(a_ref[...], w_ref[:, : 3 * heads_dim], 1, 0).astype(BF)

    rows = pl.ds(pl.multiple_of(step * BLOCK, BLOCK), BLOCK)
    parts = []
    for head in range(heads):
        low = head * DH
        query = qkv_ref[rows, low : low + DH] * BF(DH**-0.5)
        key_rows = qkv_ref[:, heads_dim + low : heads_dim + low + DH]
        value_rows = qkv_ref[:, 2 * heads_dim + low : 2 * heads_dim + low + DH]
        scores = dot(query, key_rows, 1, 1)
        expon = jnp.exp(scores - jnp.max(scores, -1, keepdims=True))
        total = jnp.sum(expon, -1, keepdims=True)
        probs = (expon * (1.0 / total)).astype(BF)
        parts.append(dot(probs, value_rows, 1, 0))
    mixed = jnp.concatenate(parts, -1).astype(BF)
    mixed_ref[...] = mixed
    part_ref[...] = dot(mixed, w_ref[:, 3 * heads_dim : 4 * heads_dim], 1, 1).astype(BF)


def attend_ahead(a_rows, w_pack, heads_dim):
    tokens, width = a_rows.shape
    return pl.pallas_call(
        attend_ahead_body,
        grid=(tokens // BLOCK,),
        in_specs=[whole_spec(a_rows), whole_spec(w_pack)],
        out_specs=[
            pl.BlockSpec((BLOCK, width), lambda i: (i, 0)),
            pl.BlockSpec((tokens, 3 * heads_dim), lambda i: (0, 0)),
            pl.BlockSpec((BLOCK, heads_dim), lambda i: (i, 0)),
        ],
        out_shape=[
            jax.ShapeDtypeStruct((tokens, width), BF),
            jax.ShapeDtypeStruct((tokens, 3 * heads_dim), BF),
            jax.ShapeDtypeStruct((tokens, heads_dim), BF),
        ],
        compiler_params=params(),
        cost_estimate=pl.CostEstimate(
            flops=2 * tokens * heads_dim * (4 * width + 4 * 2 * tokens),
            bytes_accessed=8 * 1024 * 1024,
            transcendentals=tokens * tokens * heads_dim // DH,
        ),
    )(a_rows, w_pack)


def attend_behind_body(
    da_ref, a_ref, qkv_ref, mixed_ref, w_ref, back_ref, grad_ref, dqkv_ref, acc_ref
):
    step = pl.program_id(0)
    heads_dim = mixed_ref.shape[1]
    heads = heads_dim // DH

    @pl.when(step == 0)
    def _():
        acc_ref[...] = jnp.zeros_like(acc_ref)

    rows = pl.ds(pl.multiple_of(step * BLOCK, BLOCK), BLOCK)
    d_mixed = dot(da_ref[rows, :], w_ref[:, 3 * heads_dim : 4 * heads_dim], 1, 0).astype(BF)
    query_parts = []
    key_parts = []
    value_parts = []
    for head in range(heads):
        low = head * DH
        query = qkv_ref[rows, low : low + DH]
        key_rows = qkv_ref[:, heads_dim + low : heads_dim + low + DH]
        value_rows = qkv_ref[:, 2 * heads_dim + low : 2 * heads_dim + low + DH]
        d_mixed_one = d_mixed[:, low : low + DH]
        scores = dot(key_rows, query * BF(DH**-0.5), 1, 1)
        expon = jnp.exp(scores - jnp.max(scores, 0, keepdims=True))
        probs = expon * (1.0 / jnp.sum(expon, 0, keepdims=True))
        d_probs = dot(value_rows, d_mixed_one, 1, 1)
        weighted = probs * d_probs
        d_scores = weighted - probs * jnp.sum(weighted, 0, keepdims=True)
        d_scaled = (d_scores * (DH**-0.5)).astype(BF)
        query_parts.append(dot(d_scaled, key_rows, 0, 0))
        key_parts.append(dot(d_scaled, query, 1, 0))
        value_parts.append(dot(probs.astype(BF), d_mixed_one, 1, 0))
    dqkv_ref[rows, :heads_dim] = jnp.concatenate(query_parts, -1).astype(BF)
    acc_ref[...] += jnp.concatenate(key_parts + value_parts, -1)

    @pl.when(step == pl.num_programs(0) - 1)
    def _():
        dqkv_ref[:, heads_dim:] = acc_ref[...].astype(BF)
        back_ref[...] = dot(dqkv_ref[...], w_ref[:, : 3 * heads_dim], 1, 1).astype(BF)
        grad_ref[:, : 3 * heads_dim] = dot(a_ref[...], dqkv_ref[...], 0, 0).astype(BF)
        grad_ref[:, 3 * heads_dim :] = dot(da_ref[...], mixed_ref[...], 0, 0).astype(BF)


def attend_behind(da_rows, a_rows, qkv, mixed, w_pack):
    tokens, width = a_rows.shape
    heads_dim = mixed.shape[1]
    operands = (da_rows, a_rows, qkv, mixed, w_pack)
    return pl.pallas_call(
        attend_behind_body,
        grid=(tokens // BLOCK,),
        in_specs=[whole_spec(operand) for operand in operands],
        out_specs=[
            pl.BlockSpec((tokens, width), lambda i: (0, 0)),
            pl.BlockSpec((width, 4 * heads_dim), lambda i: (0, 0)),
        ],
        out_shape=[
            jax.ShapeDtypeStruct((tokens, width), BF),
            jax.ShapeDtypeStruct((width, 4 * heads_dim), BF),
        ],
        scratch_shapes=[
            pltpu.VMEM((tokens, 3 * heads_dim), BF),
            pltpu.VMEM((tokens, 2 * heads_dim), F32),
        ],
        compiler_params=params(),
        cost_estimate=pl.CostEstimate(
            flops=2 * tokens * heads_dim * (8 * width + 4 * 5 * tokens),
            bytes_accessed=10 * 1024 * 1024,
            transcendentals=tokens * tokens * heads_dim // DH,
        ),
    )(*operands)


def pick_rows(position_ref, step, capacity):
    tokens = position_ref.shape[1]
    slot = lax.broadcasted_iota(jnp.int32, (capacity, tokens), 0) + step * capacity
    return jnp.where(slot == position_ref[...], 1.0, 0.0).astype(BF)


def place_rows(position_ref, slots_total):
    tokens = position_ref.shape[0]
    slot = lax.broadcasted_iota(jnp.int32, (tokens, slots_total), 1)
    return jnp.where(slot == position_ref[...], 1.0, 0.0).astype(BF)


def experts_ahead_body(b_ref, row_ref, col_ref, w_ref, out_ref, buffer_ref, pre_ref, eo_ref):
    step = pl.program_id(0)
    capacity, hidden = pre_ref.shape
    buffer = dot(pick_rows(row_ref, step, capacity), b_ref[...], 1, 0).astype(BF)
    buffer_ref[...] = buffer
    pre = dot(buffer, w_ref[:, :hidden], 1, 0)
    pre_ref[...] = pre
    act = (0.5 * pre * (1.0 + jnp.tanh(GELU_C * (pre + GELU_A * pre * pre * pre)))).astype(BF)
    rows = pl.ds(pl.multiple_of(step * capacity, capacity), capacity)
    eo_ref[rows, :] = dot(act, w_ref[:, hidden:], 1, 1).astype(BF)

    @pl.when(step == pl.num_programs(0) - 1)
    def _():
        place = place_rows(col_ref, eo_ref.shape[0])
        out_ref[...] = dot(place, eo_ref[...], 1, 0).astype(BF)


def experts_ahead(b_rows, pos_row, pos_col, w_pack, experts, capacity):
    tokens, width = b_rows.shape
    both = w_pack.shape[1] // experts
    hidden = both // 2
    slots_total = experts * capacity
    return pl.pallas_call(
        experts_ahead_body,
        grid=(experts,),
        in_specs=[
            whole_spec(b_rows),
            whole_spec(pos_row),
            whole_spec(pos_col),
            pl.BlockSpec((width, both), lambda i: (0, i)),
        ],
        out_specs=[
            pl.BlockSpec((tokens, width), lambda i: (0, 0)),
            pl.BlockSpec((capacity, width), lambda i: (i, 0)),
            pl.BlockSpec((capacity, hidden), lambda i: (i, 0)),
        ],
        out_shape=[
            jax.ShapeDtypeStruct((tokens, width), BF),
            jax.ShapeDtypeStruct((slots_total, width), BF),
            jax.ShapeDtypeStruct((slots_total, hidden), F32),
        ],
        scratch_shapes=[pltpu.VMEM((slots_total, width), BF)],
        compiler_params=params(),
        cost_estimate=pl.CostEstimate(
            flops=2 * slots_total * width * (2 * hidden + 2 * tokens),
            bytes_accessed=20 * 1024 * 1024,
            transcendentals=slots_total * hidden,
        ),
    )(b_rows, pos_row, pos_col, w_pack)


def experts_behind_body(
    dc_ref, row_ref, col_ref, buffer_ref, pre_ref, w_ref, back_ref, grad_ref, db_ref
):
    step = pl.program_id(0)
    capacity, hidden = pre_ref.shape
    d_out = dot(pick_rows(row_ref, step, capacity), dc_ref[...], 1, 0).astype(BF)
    pre = pre_ref[...]
    squared = pre * pre
    bent = jnp.tanh(GELU_C * (pre + GELU_A * squared * pre))
    half = 0.5 * (1.0 + bent)
    act = (pre * half).astype(BF)
    grad_ref[:, hidden:] = dot(d_out, act, 0, 0).astype(BF)
    slope = half + 0.5 * pre * (1.0 - bent * bent) * (GELU_C * (1.0 + 3.0 * GELU_A * squared))
    d_pre = (dot(d_out, w_ref[:, hidden:], 1, 0) * slope).astype(BF)
    grad_ref[:, :hidden] = dot(buffer_ref[...], d_pre, 0, 0).astype(BF)
    rows = pl.ds(pl.multiple_of(step * capacity, capacity), capacity)
    db_ref[rows, :] = dot(d_pre, w_ref[:, :hidden], 1, 1).astype(BF)

    @pl.when(step == pl.num_programs(0) - 1)
    def _():
        place = place_rows(col_ref, db_ref.shape[0])
        back_ref[...] = dot(place, db_ref[...], 1, 0).astype(BF)


def experts_behind(dc_rows, pos_row, pos_col, buffer, pre, w_pack, experts, capacity):
    tokens, width = dc_rows.shape
    both = w_pack.shape[1] // experts
    hidden = both // 2
    slots_total = experts * capacity
    return pl.pallas_call(
        experts_behind_body,
        grid=(experts,),
        in_specs=[
            whole_spec(dc_rows),
            whole_spec(pos_row),
            whole_spec(pos_col),
            pl.BlockSpec((capacity, width), lambda i: (i, 0)),
            pl.BlockSpec((capacity, hidden), lambda i: (i, 0)),
            pl.BlockSpec((width, both), lambda i: (0, i)),
        ],
        out_specs=[
            pl.BlockSpec((tokens, width), lambda i: (0, 0)),
            pl.BlockSpec((width, both), lambda i: (0, i)),
        ],
        out_shape=[
            jax.ShapeDtypeStruct((tokens, width), BF),
            jax.ShapeDtypeStruct((width, experts * both), BF),
        ],
        scratch_shapes=[pltpu.VMEM((slots_total, width), BF)],
        compiler_params=params(),
        cost_estimate=pl.CostEstimate(
            flops=2 * slots_total * width * (4 * hidden + 2 * tokens),
            bytes_accessed=30 * 1024 * 1024,
            transcendentals=slots_total * hidden,
        ),
    )(dc_rows, pos_row, pos_col, buffer, pre, w_pack)


MESH = pl.DeviceIdType.MESH
SUB = 2


def greet(me, count):
    barrier = pltpu.get_barrier_semaphore()

    @pl.when(me > 0)
    def _():
        pl.semaphore_signal(barrier, inc=1, device_id={"tp": me - 1}, device_id_type=MESH)

    @pl.when(me < count - 1)
    def _():
        pl.semaphore_signal(barrier, inc=1, device_id={"tp": me + 1}, device_id_type=MESH)

    inside = (me > 0) & (me < count - 1)

    @pl.when(inside)
    def _():
        pl.semaphore_wait(barrier, 2)

    @pl.when(jnp.logical_not(inside))
    def _():
        pl.semaphore_wait(barrier, 1)


def gather_body(count, part_ref, out_ref, own_sem, send_sem, recv_sem):
    me = lax.axis_index("tp")
    piece = part_ref.shape[0] // SUB
    own = pltpu.make_async_copy(
        part_ref, out_ref.at[pl.ds(pl.multiple_of(me * piece * SUB, piece), piece * SUB)], own_sem
    )
    own.start()
    greet(me, count)

    def copy(way, step, sub):
        sign = 1 - 2 * way
        chunk = me - sign * step
        place = pl.ds(pl.multiple_of((chunk * SUB + sub) * piece, piece), piece)
        source = part_ref.at[pl.ds(sub * piece, piece)] if step == 0 else out_ref.at[place]
        return pltpu.make_async_remote_copy(
            src_ref=source,
            dst_ref=out_ref.at[place],
            send_sem=send_sem.at[way, step, sub],
            recv_sem=recv_sem.at[way, step, sub],
            device_id={"tp": me + sign},
            device_id_type=MESH,
        )

    def arrived(way, step, sub):
        sign = 1 - 2 * way
        chunk = me - sign * (step + 1)
        place = pl.ds(pl.multiple_of((chunk * SUB + sub) * piece, piece), piece)
        pltpu.make_async_remote_copy(
            src_ref=out_ref.at[place],
            dst_ref=out_ref.at[place],
            send_sem=send_sem.at[way, step, sub],
            recv_sem=recv_sem.at[way, step, sub],
            device_id={"tp": me - sign},
            device_id_type=MESH,
        ).wait_recv()

    def has(way, step):
        return me >= step if way == 0 else me + step <= count - 1

    def sends(way, step):
        return has(way, step) & (me < count - 1 if way == 0 else me > 0)

    for step in range(count):
        for sub in range(SUB):
            for way in range(2):
                if step > 0:

                    @pl.when(has(way, step))
                    def _():
                        arrived(way, step - 1, sub)

                if step < count - 1:

                    @pl.when(sends(way, step))
                    def _():
                        copy(way, step, sub).start()

    for step in range(count - 1):
        for sub in range(SUB):
            for way in range(2):

                @pl.when(sends(way, step))
                def _():
                    copy(way, step, sub).wait_send()

    own.wait()


def gather_tokens(part):
    count = lax.axis_size("tp")
    tokens, width = part.shape
    return pl.pallas_call(
        functools.partial(gather_body, count),
        in_specs=[pl.BlockSpec(memory_space=pl.ANY)],
        out_specs=pl.BlockSpec(memory_space=pl.ANY),
        out_shape=jax.ShapeDtypeStruct((count * tokens, width), part.dtype),
        scratch_shapes=[
            pltpu.SemaphoreType.DMA,
            pltpu.SemaphoreType.DMA((2, count - 1, SUB)),
            pltpu.SemaphoreType.DMA((2, count - 1, SUB)),
        ],
        compiler_params=pltpu.CompilerParams(collective_id=0, has_side_effects=True),
        cost_estimate=pl.CostEstimate(flops=0, bytes_accessed=80 * 1024 * 1024, transcendentals=0),
    )(part)


def scatter_body(count, whole_ref, out_ref, held_ref, sent_ref, send_sem, recv_sem):
    me = lax.axis_index("tp")
    tokens = out_ref.shape[0]
    piece = tokens // SUB
    greet(me, count)

    def rows(chunk, sub):
        return pl.ds(pl.multiple_of(chunk * tokens + sub * piece, piece), piece)

    def copy(way, step, sub):
        sign = 1 - 2 * way
        return pltpu.make_async_remote_copy(
            src_ref=sent_ref.at[way, step, pl.ds(sub * piece, piece)],
            dst_ref=held_ref.at[way, step, pl.ds(sub * piece, piece)],
            send_sem=send_sem.at[way, step, sub],
            recv_sem=recv_sem.at[way, step, sub],
            device_id={"tp": me + sign},
            device_id_type=MESH,
        )

    def goes(way, chunk):
        return me < chunk if way == 0 else me > chunk

    def first(way):
        return me == 0 if way == 0 else me == count - 1

    for sub in range(SUB):
        out_ref[sub * piece : (sub + 1) * piece, :] = whole_ref[rows(me, sub), :].astype(F32)
    for step in range(count - 1):
        for sub in range(SUB):
            for way in range(2):
                chunk = count - 1 - step if way == 0 else step
                part = pl.ds(sub * piece, piece)

                @pl.when(goes(way, chunk) & first(way))
                def _():
                    sent_ref[way, step, part, :] = whole_ref[rows(chunk, sub), :]
                    copy(way, step, sub).start()

                @pl.when(goes(way, chunk) & jnp.logical_not(first(way)))
                def _():
                    copy(way, step, sub).wait_recv()
                    total = whole_ref[rows(chunk, sub), :].astype(F32)
                    total = total + held_ref[way, step, part, :].astype(F32)
                    sent_ref[way, step, part, :] = total.astype(BF)
                    copy(way, step, sub).start()

                @pl.when((me == chunk) & jnp.logical_not(first(way)))
                def _():
                    copy(way, step, sub).wait_recv()
                    out_ref[part, :] += held_ref[way, step, part, :].astype(F32)

    for step in range(count - 1):
        for sub in range(SUB):
            for way in range(2):
                chunk = count - 1 - step if way == 0 else step

                @pl.when(goes(way, chunk))
                def _():
                    copy(way, step, sub).wait_send()


def scatter_tokens(whole):
    count = lax.axis_size("tp")
    tokens, width = whole.shape[0] // count, whole.shape[1]
    return pl.pallas_call(
        functools.partial(scatter_body, count),
        in_specs=[pl.BlockSpec(memory_space=pltpu.VMEM)],
        out_specs=pl.BlockSpec(memory_space=pltpu.VMEM),
        out_shape=jax.ShapeDtypeStruct((tokens, width), F32),
        scratch_shapes=[
            pltpu.VMEM((2, count - 1, tokens, width), BF),
            pltpu.VMEM((2, count - 1, tokens, width), BF),
            pltpu.SemaphoreType.DMA((2, count - 1, SUB)),
            pltpu.SemaphoreType.DMA((2, count - 1, SUB)),
        ],
        compiler_params=pltpu.CompilerParams(
            collective_id=1, has_side_effects=True, vmem_limit_bytes=24 * 1024 * 1024
        ),
        cost_estimate=pl.CostEstimate(flops=0, bytes_accessed=80 * 1024 * 1024, transcendentals=0),
    )(whole)


def local(
    inputs,
    cotangent,
    qkv_weight,
    out_weight,
    attn_gain,
    ffn_gain,
    router_weight,
    in_weight,
    down_weight,
    routes,
    slots,
):
    tp_index = lax.axis_index("tp")
    fsdp_index = lax.axis_index("fsdp")
    tok_here, width = inputs.shape
    shard = in_weight.shape[2]
    experts = in_weight.shape[1]
    hidden_units = in_weight.shape[3]
    heads_dim = qkv_weight.shape[3]
    group_tok = routes.shape[0]
    capacity = group_tok // experts

    packs = []
    for layer_index in range(LAYERS):
        small = [
            jnp.transpose(qkv_weight[layer_index], (1, 0, 2)).reshape(shard, 3 * heads_dim),
            out_weight[layer_index].T,
            attn_gain[layer_index][:, None],
            ffn_gain[layer_index][:, None],
            router_weight[layer_index],
        ]
        columns = 4 * heads_dim + 2 + experts
        small.append(jnp.zeros((shard, -columns % 128), BF))
        large = jnp.stack(
            [in_weight[layer_index], jnp.transpose(down_weight[layer_index], (0, 2, 1))], 1
        )
        large = jnp.transpose(large, (2, 0, 1, 3)).reshape(shard, experts * 2 * hidden_units)
        packs.append(
            (
                lax.all_gather(jnp.concatenate(small, 1), "fsdp", axis=0, tiled=True),
                lax.all_gather(large, "fsdp", axis=0, tiled=True),
            )
        )

    position = jnp.where(slots < capacity, routes * capacity + slots, -1)
    pos_row, pos_col = position[None, :], position[:, None]
    route_here = lax.dynamic_slice_in_dim(routes, tp_index * tok_here, tok_here)
    pick = (route_here[:, None] == jnp.arange(experts, dtype=jnp.int32)[None, :]).astype(F32)
    hidden = inputs.astype(F32)
    saved = []
    for layer_index in range(LAYERS):
        w_attn, w_experts = packs[layer_index]
        rest = w_attn[:, 4 * heads_dim : 4 * heads_dim + 2 + experts]
        rest_rows = rest.astype(F32).T
        gain_one, gain_two, router_rows = rest_rows[0], rest_rows[1], rest_rows[2:]
        a_here = normed(hidden, gain_one).astype(BF)
        a_rows = gather_tokens(a_here)
        partial_attn, qkv, mixed = attend_ahead(a_rows, w_attn, heads_dim)
        middle = hidden + scatter_tokens(partial_attn)
        b_here = normed(middle, gain_two).astype(BF)
        b_rows = gather_tokens(b_here)
        logits = jnp.dot(b_here, rest[:, 2:], preferred_element_type=F32)
        probs = jax.nn.softmax(logits, -1)
        gate = jnp.sum(probs * pick, -1)
        token_out, buffer, pre = experts_ahead(
            b_rows, pos_row, pos_col, w_experts, experts, capacity
        )
        combined = scatter_tokens(token_out)
        saved.append(
            (gain_one, gain_two, router_rows, hidden, a_rows, qkv, mixed, middle)
            + (b_here, probs, gate, combined, buffer, pre)
        )
        hidden = middle + gate[:, None] * combined
    upstream = cotangent.astype(F32)
    layer_grads = [None] * LAYERS
    small_sums = [None] * LAYERS
    for layer_index in reversed(range(LAYERS)):
        w_attn, w_experts = packs[layer_index]
        (gain_one, gain_two, router_rows, before, a_rows, qkv, mixed, middle) = saved[layer_index][:8]
        (b_here, probs, gate, combined, buffer, pre) = saved[layer_index][8:]
        dc_rows = gather_tokens((gate[:, None] * upstream).astype(BF))
        d_gate = jnp.sum(upstream * combined, -1)
        d_tokens, grad_experts = experts_behind(
            dc_rows, pos_row, pos_col, buffer, pre, w_experts, experts, capacity
        )
        d_logits = d_gate[:, None] * gate[:, None] * (pick - probs)
        d_b_here = scatter_tokens(d_tokens)
        for expert in range(experts):
            d_b_here = d_b_here + d_logits[:, expert : expert + 1] * router_rows[expert][None, :]
        grad_router = lax.dot_general(
            d_logits, b_here.astype(F32), (((0,), (0,)), ((), ())), precision=HIGH
        )
        d_middle, grad_gain_two = normed_back(middle, gain_two, d_b_here)
        d_middle = d_middle + upstream
        da_rows = gather_tokens(d_middle.astype(BF))
        d_a_rows, grad_attn = attend_behind(da_rows, a_rows, qkv, mixed, w_attn)
        d_before, grad_gain_one = normed_back(before, gain_one, scatter_tokens(d_a_rows))
        upstream = d_before + d_middle
        layer_grads[layer_index] = (
            lax.psum_scatter(grad_attn, "fsdp", scatter_dimension=0, tiled=True),
            lax.psum_scatter(grad_experts, "fsdp", scatter_dimension=0, tiled=True),
        )
        small_sums[layer_index] = jnp.concatenate(
            [grad_gain_one[None], grad_gain_two[None], grad_router], 0
        )
    sums = lax.psum(jnp.concatenate(small_sums, 0), ("fsdp", "tp"))
    sums = lax.dynamic_slice_in_dim(sums, fsdp_index * shard, shard, 1)
    sums = sums.reshape(LAYERS, 2 + experts, shard)
    attn_grads = jnp.stack([grads[0] for grads in layer_grads]).astype(F32)
    expert_grads = jnp.stack([grads[1] for grads in layer_grads]).astype(F32)
    expert_grads = expert_grads.reshape(LAYERS, shard, experts, 2, hidden_units)
    qkv_grads = attn_grads[:, :, : 3 * heads_dim].reshape(LAYERS, shard, 3, heads_dim)
    return (
        hidden,
        upstream,
        jnp.transpose(qkv_grads, (0, 2, 1, 3)),
        jnp.transpose(attn_grads[:, :, 3 * heads_dim :], (0, 2, 1)),
        sums[:, 0],
        sums[:, 1],
        jnp.transpose(sums[:, 2:], (0, 2, 1)),
        jnp.transpose(expert_grads[:, :, :, 0], (0, 2, 1, 3)),
        jnp.transpose(expert_grads[:, :, :, 1], (0, 2, 3, 1)),
    )


def solution(mesh):
    return jax.shard_map(
        local,
        mesh=mesh,
        in_specs=(
            P(("fsdp", "tp"), None),
            P(("fsdp", "tp"), None),
            P(None, None, "fsdp", "tp"),
            P(None, "tp", "fsdp"),
            P(None, "fsdp"),
            P(None, "fsdp"),
            P(None, "fsdp", None),
            P(None, None, "fsdp", "tp"),
            P(None, None, "tp", "fsdp"),
            P("fsdp"),
            P("fsdp"),
        ),
        out_specs=(
            P(("fsdp", "tp"), None),
            P(("fsdp", "tp"), None),
            P(None, None, "fsdp", "tp"),
            P(None, "tp", "fsdp"),
            P(None, "fsdp"),
            P(None, "fsdp"),
            P(None, "fsdp", None),
            P(None, None, "fsdp", "tp"),
            P(None, None, "tp", "fsdp"),
        ),
        check_vma=False,
    )
```

```python
import functools

import jax
import jax.numpy as jnp
from jax import lax
from jax.experimental import pallas as pl
from jax.experimental.pallas import tpu as pltpu
from jax.sharding import PartitionSpec as P

DH = 64
LAYERS = 2
BLOCK = 256

EPSILON = 1e-06
HIGH = lax.Precision.HIGHEST
BF = jnp.bfloat16
F32 = jnp.float32
GELU_C = 0.7978845608028654
GELU_A = 0.044715
VMEM_BYTES = 48 * 1024 * 1024


def dot(left, right, left_dim, right_dim):
    return lax.dot_general(
        left, right, (((left_dim,), (right_dim,)), ((), ())), preferred_element_type=F32
    )


def normed(hidden, gain_row):
    scale_inv = lax.rsqrt(jnp.mean(hidden * hidden, -1, keepdims=True) + EPSILON)
    return hidden * scale_inv * gain_row


def normed_back(hidden, gain_row, upstream):
    _, pull_back = jax.vjp(normed, hidden, gain_row)
    return pull_back(upstream)


def params():
    return pltpu.CompilerParams(
        dimension_semantics=("arbitrary",), vmem_limit_bytes=VMEM_BYTES
    )


def whole_spec(array):
    rank = len(array.shape)
    return pl.BlockSpec(array.shape, lambda i: (0,) * rank)


def attend_ahead_body(a_ref, w_ref, part_ref, qkv_ref, mixed_ref):
    step = pl.program_id(0)
    heads_dim = mixed_ref.shape[1]
    heads = heads_dim // DH

    @pl.when(step == 0)
    def _():
        qkv_ref[...] = dot(a_ref[...], w_ref[:, : 3 * heads_dim], 1, 0).astype(BF)

    rows = pl.ds(pl.multiple_of(step * BLOCK, BLOCK), BLOCK)
    parts = []
    for head in range(heads):
        low = head * DH
        query = qkv_ref[rows, low : low + DH] * BF(DH**-0.5)
        key_rows = qkv_ref[:, heads_dim + low : heads_dim + low + DH]
        value_rows = qkv_ref[:, 2 * heads_dim + low : 2 * heads_dim + low + DH]
        scores = dot(query, key_rows, 1, 1)
        expon = jnp.exp(scores - jnp.max(scores, -1, keepdims=True))
        total = jnp.sum(expon, -1, keepdims=True)
        probs = (expon * (1.0 / total)).astype(BF)
        parts.append(dot(probs, value_rows, 1, 0))
    mixed = jnp.concatenate(parts, -1).astype(BF)
    mixed_ref[...] = mixed
    part_ref[...] = dot(mixed, w_ref[:, 3 * heads_dim : 4 * heads_dim], 1, 1).astype(BF)


def attend_ahead(a_rows, w_pack, heads_dim):
    tokens, width = a_rows.shape
    return pl.pallas_call(
        attend_ahead_body,
        grid=(tokens // BLOCK,),
        in_specs=[whole_spec(a_rows), whole_spec(w_pack)],
        out_specs=[
            pl.BlockSpec((BLOCK, width), lambda i: (i, 0)),
            pl.BlockSpec((tokens, 3 * heads_dim), lambda i: (0, 0)),
            pl.BlockSpec((BLOCK, heads_dim), lambda i: (i, 0)),
        ],
        out_shape=[
            jax.ShapeDtypeStruct((tokens, width), BF),
            jax.ShapeDtypeStruct((tokens, 3 * heads_dim), BF),
            jax.ShapeDtypeStruct((tokens, heads_dim), BF),
        ],
        compiler_params=params(),
        cost_estimate=pl.CostEstimate(
            flops=2 * tokens * heads_dim * (4 * width + 4 * 2 * tokens),
            bytes_accessed=8 * 1024 * 1024,
            transcendentals=tokens * tokens * heads_dim // DH,
        ),
    )(a_rows, w_pack)


def attend_behind_body(
    da_ref, a_ref, qkv_ref, mixed_ref, w_ref, back_ref, grad_ref, dqkv_ref, acc_ref
):
    step = pl.program_id(0)
    heads_dim = mixed_ref.shape[1]
    heads = heads_dim // DH

    @pl.when(step == 0)
    def _():
        acc_ref[...] = jnp.zeros_like(acc_ref)

    rows = pl.ds(pl.multiple_of(step * BLOCK, BLOCK), BLOCK)
    d_mixed = dot(da_ref[rows, :], w_ref[:, 3 * heads_dim : 4 * heads_dim], 1, 0).astype(BF)
    query_parts = []
    key_parts = []
    value_parts = []
    for head in range(heads):
        low = head * DH
        query = qkv_ref[rows, low : low + DH]
        key_rows = qkv_ref[:, heads_dim + low : heads_dim + low + DH]
        value_rows = qkv_ref[:, 2 * heads_dim + low : 2 * heads_dim + low + DH]
        d_mixed_one = d_mixed[:, low : low + DH]
        scores = dot(key_rows, query * BF(DH**-0.5), 1, 1)
        expon = jnp.exp(scores - jnp.max(scores, 0, keepdims=True))
        probs = expon * (1.0 / jnp.sum(expon, 0, keepdims=True))
        d_probs = dot(value_rows, d_mixed_one, 1, 1)
        weighted = probs * d_probs
        d_scores = weighted - probs * jnp.sum(weighted, 0, keepdims=True)
        d_scaled = (d_scores * (DH**-0.5)).astype(BF)
        query_parts.append(dot(d_scaled, key_rows, 0, 0))
        key_parts.append(dot(d_scaled, query, 1, 0))
        value_parts.append(dot(probs.astype(BF), d_mixed_one, 1, 0))
    dqkv_ref[rows, :heads_dim] = jnp.concatenate(query_parts, -1).astype(BF)
    acc_ref[...] += jnp.concatenate(key_parts + value_parts, -1)

    @pl.when(step == pl.num_programs(0) - 1)
    def _():
        dqkv_ref[:, heads_dim:] = acc_ref[...].astype(BF)
        back_ref[...] = dot(dqkv_ref[...], w_ref[:, : 3 * heads_dim], 1, 1).astype(BF)
        grad_ref[:, : 3 * heads_dim] = dot(a_ref[...], dqkv_ref[...], 0, 0).astype(BF)
        grad_ref[:, 3 * heads_dim :] = dot(da_ref[...], mixed_ref[...], 0, 0).astype(BF)


def attend_behind(da_rows, a_rows, qkv, mixed, w_pack):
    tokens, width = a_rows.shape
    heads_dim = mixed.shape[1]
    operands = (da_rows, a_rows, qkv, mixed, w_pack)
    return pl.pallas_call(
        attend_behind_body,
        grid=(tokens // BLOCK,),
        in_specs=[whole_spec(operand) for operand in operands],
        out_specs=[
            pl.BlockSpec((tokens, width), lambda i: (0, 0)),
            pl.BlockSpec((width, 4 * heads_dim), lambda i: (0, 0)),
        ],
        out_shape=[
            jax.ShapeDtypeStruct((tokens, width), BF),
            jax.ShapeDtypeStruct((width, 4 * heads_dim), BF),
        ],
        scratch_shapes=[
            pltpu.VMEM((tokens, 3 * heads_dim), BF),
            pltpu.VMEM((tokens, 2 * heads_dim), F32),
        ],
        compiler_params=params(),
        cost_estimate=pl.CostEstimate(
            flops=2 * tokens * heads_dim * (8 * width + 4 * 5 * tokens),
            bytes_accessed=10 * 1024 * 1024,
            transcendentals=tokens * tokens * heads_dim // DH,
        ),
    )(*operands)


def pick_rows(position_ref, step, capacity):
    tokens = position_ref.shape[1]
    slot = lax.broadcasted_iota(jnp.int32, (capacity, tokens), 0) + step * capacity
    return jnp.where(slot == position_ref[...], 1.0, 0.0).astype(BF)


def place_rows(position_ref, slots_total):
    tokens = position_ref.shape[0]
    slot = lax.broadcasted_iota(jnp.int32, (tokens, slots_total), 1)
    return jnp.where(slot == position_ref[...], 1.0, 0.0).astype(BF)


def experts_ahead_body(b_ref, row_ref, col_ref, w_ref, out_ref, buffer_ref, pre_ref, eo_ref):
    step = pl.program_id(0)
    capacity, hidden = pre_ref.shape
    buffer = dot(pick_rows(row_ref, step, capacity), b_ref[...], 1, 0).astype(BF)
    buffer_ref[...] = buffer
    pre = dot(buffer, w_ref[:, :hidden], 1, 0)
    pre_ref[...] = pre
    act = (0.5 * pre * (1.0 + jnp.tanh(GELU_C * (pre + GELU_A * pre * pre * pre)))).astype(BF)
    rows = pl.ds(pl.multiple_of(step * capacity, capacity), capacity)
    eo_ref[rows, :] = dot(act, w_ref[:, hidden:], 1, 1).astype(BF)

    @pl.when(step == pl.num_programs(0) - 1)
    def _():
        place = place_rows(col_ref, eo_ref.shape[0])
        out_ref[...] = dot(place, eo_ref[...], 1, 0).astype(BF)


def experts_ahead(b_rows, pos_row, pos_col, w_pack, experts, capacity):
    tokens, width = b_rows.shape
    both = w_pack.shape[1] // experts
    hidden = both // 2
    slots_total = experts * capacity
    return pl.pallas_call(
        experts_ahead_body,
        grid=(experts,),
        in_specs=[
            whole_spec(b_rows),
            whole_spec(pos_row),
            whole_spec(pos_col),
            pl.BlockSpec((width, both), lambda i: (0, i)),
        ],
        out_specs=[
            pl.BlockSpec((tokens, width), lambda i: (0, 0)),
            pl.BlockSpec((capacity, width), lambda i: (i, 0)),
            pl.BlockSpec((capacity, hidden), lambda i: (i, 0)),
        ],
        out_shape=[
            jax.ShapeDtypeStruct((tokens, width), BF),
            jax.ShapeDtypeStruct((slots_total, width), BF),
            jax.ShapeDtypeStruct((slots_total, hidden), F32),
        ],
        scratch_shapes=[pltpu.VMEM((slots_total, width), BF)],
        compiler_params=params(),
        cost_estimate=pl.CostEstimate(
            flops=2 * slots_total * width * (2 * hidden + 2 * tokens),
            bytes_accessed=20 * 1024 * 1024,
            transcendentals=slots_total * hidden,
        ),
    )(b_rows, pos_row, pos_col, w_pack)


def experts_behind_body(
    dc_ref, row_ref, col_ref, buffer_ref, pre_ref, w_ref, back_ref, grad_ref, db_ref
):
    step = pl.program_id(0)
    capacity, hidden = pre_ref.shape
    d_out = dot(pick_rows(row_ref, step, capacity), dc_ref[...], 1, 0).astype(BF)
    pre = pre_ref[...]
    squared = pre * pre
    bent = jnp.tanh(GELU_C * (pre + GELU_A * squared * pre))
    half = 0.5 * (1.0 + bent)
    act = (pre * half).astype(BF)
    grad_ref[:, hidden:] = dot(d_out, act, 0, 0).astype(BF)
    slope = half + 0.5 * pre * (1.0 - bent * bent) * (GELU_C * (1.0 + 3.0 * GELU_A * squared))
    d_pre = (dot(d_out, w_ref[:, hidden:], 1, 0) * slope).astype(BF)
    grad_ref[:, :hidden] = dot(buffer_ref[...], d_pre, 0, 0).astype(BF)
    rows = pl.ds(pl.multiple_of(step * capacity, capacity), capacity)
    db_ref[rows, :] = dot(d_pre, w_ref[:, :hidden], 1, 1).astype(BF)

    @pl.when(step == pl.num_programs(0) - 1)
    def _():
        place = place_rows(col_ref, db_ref.shape[0])
        back_ref[...] = dot(place, db_ref[...], 1, 0).astype(BF)


def experts_behind(dc_rows, pos_row, pos_col, buffer, pre, w_pack, experts, capacity):
    tokens, width = dc_rows.shape
    both = w_pack.shape[1] // experts
    hidden = both // 2
    slots_total = experts * capacity
    return pl.pallas_call(
        experts_behind_body,
        grid=(experts,),
        in_specs=[
            whole_spec(dc_rows),
            whole_spec(pos_row),
            whole_spec(pos_col),
            pl.BlockSpec((capacity, width), lambda i: (i, 0)),
            pl.BlockSpec((capacity, hidden), lambda i: (i, 0)),
            pl.BlockSpec((width, both), lambda i: (0, i)),
        ],
        out_specs=[
            pl.BlockSpec((tokens, width), lambda i: (0, 0)),
            pl.BlockSpec((width, both), lambda i: (0, i)),
        ],
        out_shape=[
            jax.ShapeDtypeStruct((tokens, width), BF),
            jax.ShapeDtypeStruct((width, experts * both), BF),
        ],
        scratch_shapes=[pltpu.VMEM((slots_total, width), BF)],
        compiler_params=params(),
        cost_estimate=pl.CostEstimate(
            flops=2 * slots_total * width * (4 * hidden + 2 * tokens),
            bytes_accessed=30 * 1024 * 1024,
            transcendentals=slots_total * hidden,
        ),
    )(dc_rows, pos_row, pos_col, buffer, pre, w_pack)


MESH = pl.DeviceIdType.MESH
SUB = 2


def greet(me, count):
    barrier = pltpu.get_barrier_semaphore()

    @pl.when(me > 0)
    def _():
        pl.semaphore_signal(barrier, inc=1, device_id={"tp": me - 1}, device_id_type=MESH)

    @pl.when(me < count - 1)
    def _():
        pl.semaphore_signal(barrier, inc=1, device_id={"tp": me + 1}, device_id_type=MESH)

    inside = (me > 0) & (me < count - 1)

    @pl.when(inside)
    def _():
        pl.semaphore_wait(barrier, 2)

    @pl.when(jnp.logical_not(inside))
    def _():
        pl.semaphore_wait(barrier, 1)


def gather_body(count, part_ref, out_ref, own_sem, send_sem, recv_sem):
    me = lax.axis_index("tp")
    piece = part_ref.shape[0] // SUB
    own = pltpu.make_async_copy(
        part_ref, out_ref.at[pl.ds(pl.multiple_of(me * piece * SUB, piece), piece * SUB)], own_sem
    )
    own.start()
    greet(me, count)

    def copy(way, step, sub):
        sign = 1 - 2 * way
        chunk = me - sign * step
        place = pl.ds(pl.multiple_of((chunk * SUB + sub) * piece, piece), piece)
        source = part_ref.at[pl.ds(sub * piece, piece)] if step == 0 else out_ref.at[place]
        return pltpu.make_async_remote_copy(
            src_ref=source,
            dst_ref=out_ref.at[place],
            send_sem=send_sem.at[way, step, sub],
            recv_sem=recv_sem.at[way, step, sub],
            device_id={"tp": me + sign},
            device_id_type=MESH,
        )

    def arrived(way, step, sub):
        sign = 1 - 2 * way
        chunk = me - sign * (step + 1)
        place = pl.ds(pl.multiple_of((chunk * SUB + sub) * piece, piece), piece)
        pltpu.make_async_remote_copy(
            src_ref=out_ref.at[place],
            dst_ref=out_ref.at[place],
            send_sem=send_sem.at[way, step, sub],
            recv_sem=recv_sem.at[way, step, sub],
            device_id={"tp": me - sign},
            device_id_type=MESH,
        ).wait_recv()

    def has(way, step):
        return me >= step if way == 0 else me + step <= count - 1

    def sends(way, step):
        return has(way, step) & (me < count - 1 if way == 0 else me > 0)

    for step in range(count):
        for sub in range(SUB):
            for way in range(2):
                if step > 0:

                    @pl.when(has(way, step))
                    def _():
                        arrived(way, step - 1, sub)

                if step < count - 1:

                    @pl.when(sends(way, step))
                    def _():
                        copy(way, step, sub).start()

    for step in range(count - 1):
        for sub in range(SUB):
            for way in range(2):

                @pl.when(sends(way, step))
                def _():
                    copy(way, step, sub).wait_send()

    own.wait()


def gather_tokens(part):
    count = lax.axis_size("tp")
    tokens, width = part.shape
    return pl.pallas_call(
        functools.partial(gather_body, count),
        in_specs=[pl.BlockSpec(memory_space=pl.ANY)],
        out_specs=pl.BlockSpec(memory_space=pl.ANY),
        out_shape=jax.ShapeDtypeStruct((count * tokens, width), part.dtype),
        scratch_shapes=[
            pltpu.SemaphoreType.DMA,
            pltpu.SemaphoreType.DMA((2, count - 1, SUB)),
            pltpu.SemaphoreType.DMA((2, count - 1, SUB)),
        ],
        compiler_params=pltpu.CompilerParams(collective_id=0, has_side_effects=True),
        cost_estimate=pl.CostEstimate(flops=0, bytes_accessed=80 * 1024 * 1024, transcendentals=0),
    )(part)


def scatter_body(count, whole_ref, out_ref, held_ref, sent_ref, send_sem, recv_sem):
    me = lax.axis_index("tp")
    tokens = out_ref.shape[0]
    piece = tokens // SUB
    greet(me, count)

    def rows(chunk, sub):
        return pl.ds(pl.multiple_of(chunk * tokens + sub * piece, piece), piece)

    def copy(way, step, sub):
        sign = 1 - 2 * way
        return pltpu.make_async_remote_copy(
            src_ref=sent_ref.at[way, step, pl.ds(sub * piece, piece)],
            dst_ref=held_ref.at[way, step, pl.ds(sub * piece, piece)],
            send_sem=send_sem.at[way, step, sub],
            recv_sem=recv_sem.at[way, step, sub],
            device_id={"tp": me + sign},
            device_id_type=MESH,
        )

    def first(way):
        return me == 0 if way == 0 else me == count - 1

    for sub in range(SUB):
        out_ref[sub * piece : (sub + 1) * piece, :] = whole_ref[rows(me, sub), :].astype(F32)
    for turn in range(2 * count - 2):
        for sub in range(SUB):
            for way in range(2):
                step = turn - (me if way == 0 else count - 1 - me)
                chunk = count - 1 - step if way == 0 else step
                part = pl.ds(sub * piece, piece)
                goes = (step >= 0) & (me < chunk if way == 0 else me > chunk)

                @pl.when(goes & first(way))
                def _():
                    sent_ref[way, step, part, :] = whole_ref[rows(chunk, sub), :]
                    copy(way, step, sub).start()

                @pl.when(goes & jnp.logical_not(first(way)))
                def _():
                    copy(way, step, sub).wait_recv()
                    total = whole_ref[rows(chunk, sub), :].astype(F32)
                    total = total + held_ref[way, step, part, :].astype(F32)
                    sent_ref[way, step, part, :] = total.astype(BF)
                    copy(way, step, sub).start()

    for sub in range(SUB):
        for way in range(2):
            step = count - 1 - me if way == 0 else me
            part = pl.ds(sub * piece, piece)

            @pl.when(jnp.logical_not(first(way)))
            def _():
                copy(way, step, sub).wait_recv()
                out_ref[part, :] += held_ref[way, step, part, :].astype(F32)

    for step in range(count - 1):
        for sub in range(SUB):
            for way in range(2):
                chunk = count - 1 - step if way == 0 else step

                @pl.when(me < chunk if way == 0 else me > chunk)
                def _():
                    copy(way, step, sub).wait_send()


def scatter_tokens(whole):
    count = lax.axis_size("tp")
    tokens, width = whole.shape[0] // count, whole.shape[1]
    return pl.pallas_call(
        functools.partial(scatter_body, count),
        in_specs=[pl.BlockSpec(memory_space=pltpu.VMEM)],
        out_specs=pl.BlockSpec(memory_space=pltpu.VMEM),
        out_shape=jax.ShapeDtypeStruct((tokens, width), F32),
        scratch_shapes=[
            pltpu.VMEM((2, count - 1, tokens, width), BF),
            pltpu.VMEM((2, count - 1, tokens, width), BF),
            pltpu.SemaphoreType.DMA((2, count - 1, SUB)),
            pltpu.SemaphoreType.DMA((2, count - 1, SUB)),
        ],
        compiler_params=pltpu.CompilerParams(
            collective_id=1, has_side_effects=True, vmem_limit_bytes=24 * 1024 * 1024
        ),
        cost_estimate=pl.CostEstimate(flops=0, bytes_accessed=80 * 1024 * 1024, transcendentals=0),
    )(whole)


def local(
    inputs,
    cotangent,
    qkv_weight,
    out_weight,
    attn_gain,
    ffn_gain,
    router_weight,
    in_weight,
    down_weight,
    routes,
    slots,
):
    tp_index = lax.axis_index("tp")
    fsdp_index = lax.axis_index("fsdp")
    tok_here, width = inputs.shape
    shard = in_weight.shape[2]
    experts = in_weight.shape[1]
    hidden_units = in_weight.shape[3]
    heads_dim = qkv_weight.shape[3]
    group_tok = routes.shape[0]
    capacity = group_tok // experts

    packs = []
    for layer_index in range(LAYERS):
        small = [
            jnp.transpose(qkv_weight[layer_index], (1, 0, 2)).reshape(shard, 3 * heads_dim),
            out_weight[layer_index].T,
            attn_gain[layer_index][:, None],
            ffn_gain[layer_index][:, None],
            router_weight[layer_index],
        ]
        columns = 4 * heads_dim + 2 + experts
        small.append(jnp.zeros((shard, -columns % 128), BF))
        large = jnp.stack(
            [in_weight[layer_index], jnp.transpose(down_weight[layer_index], (0, 2, 1))], 1
        )
        large = jnp.transpose(large, (2, 0, 1, 3)).reshape(shard, experts * 2 * hidden_units)
        packs.append(
            (
                lax.all_gather(jnp.concatenate(small, 1), "fsdp", axis=0, tiled=True),
                lax.all_gather(large, "fsdp", axis=0, tiled=True),
            )
        )

    position = jnp.where(slots < capacity, routes * capacity + slots, -1)
    pos_row, pos_col = position[None, :], position[:, None]
    route_here = lax.dynamic_slice_in_dim(routes, tp_index * tok_here, tok_here)
    pick = (route_here[:, None] == jnp.arange(experts, dtype=jnp.int32)[None, :]).astype(F32)
    hidden = inputs.astype(F32)
    saved = []
    for layer_index in range(LAYERS):
        w_attn, w_experts = packs[layer_index]
        rest = w_attn[:, 4 * heads_dim : 4 * heads_dim + 2 + experts]
        rest_rows = rest.astype(F32).T
        gain_one, gain_two, router_rows = rest_rows[0], rest_rows[1], rest_rows[2:]
        if layer_index == 0:
            a_rows = normed(gather_tokens(inputs).astype(F32), gain_one).astype(BF)
        else:
            a_rows = gather_tokens(normed(hidden, gain_one).astype(BF))
        partial_attn, qkv, mixed = attend_ahead(a_rows, w_attn, heads_dim)
        middle = hidden + scatter_tokens(partial_attn)
        b_here = normed(middle, gain_two).astype(BF)
        b_rows = gather_tokens(b_here)
        logits = jnp.dot(b_here, rest[:, 2:], preferred_element_type=F32)
        probs = jax.nn.softmax(logits, -1)
        gate = jnp.sum(probs * pick, -1)
        token_out, buffer, pre = experts_ahead(
            b_rows, pos_row, pos_col, w_experts, experts, capacity
        )
        combined = scatter_tokens(token_out)
        saved.append(
            (gain_one, gain_two, router_rows, hidden, a_rows, qkv, mixed, middle)
            + (b_here, probs, gate, combined, buffer, pre)
        )
        hidden = middle + gate[:, None] * combined
    upstream = cotangent.astype(F32)
    layer_grads = [None] * LAYERS
    small_sums = [None] * LAYERS
    for layer_index in reversed(range(LAYERS)):
        w_attn, w_experts = packs[layer_index]
        (gain_one, gain_two, router_rows, before, a_rows, qkv, mixed, middle) = saved[layer_index][:8]
        (b_here, probs, gate, combined, buffer, pre) = saved[layer_index][8:]
        dc_rows = gather_tokens((gate[:, None] * upstream).astype(BF))
        d_gate = jnp.sum(upstream * combined, -1)
        if layer_index < LAYERS - 1:
            dc_rows, attn_shard = lax.optimization_barrier((dc_rows, attn_shard))
            layer_grads[layer_index + 1] = (attn_shard, expert_shard)
        d_tokens, grad_experts = experts_behind(
            dc_rows, pos_row, pos_col, buffer, pre, w_experts, experts, capacity
        )
        expert_shard = lax.psum_scatter(grad_experts, "fsdp", scatter_dimension=0, tiled=True)
        d_logits = d_gate[:, None] * gate[:, None] * (pick - probs)
        d_b_here = scatter_tokens(d_tokens)
        for expert in range(experts):
            d_b_here = d_b_here + d_logits[:, expert : expert + 1] * router_rows[expert][None, :]
        grad_router = lax.dot_general(
            d_logits, b_here.astype(F32), (((0,), (0,)), ((), ())), precision=HIGH
        )
        d_middle, grad_gain_two = normed_back(middle, gain_two, d_b_here)
        d_middle = d_middle + upstream
        da_rows = gather_tokens(d_middle.astype(BF))
        d_a_rows, grad_attn = attend_behind(da_rows, a_rows, qkv, mixed, w_attn)
        d_a_rows, expert_shard = lax.optimization_barrier((d_a_rows, expert_shard))
        attn_shard = lax.psum_scatter(grad_attn, "fsdp", scatter_dimension=0, tiled=True)
        d_before, grad_gain_one = normed_back(before, gain_one, scatter_tokens(d_a_rows))
        upstream = d_before + d_middle
        small_sums[layer_index] = jnp.concatenate(
            [grad_gain_one[None], grad_gain_two[None], grad_router], 0
        )
    layer_grads[0] = (attn_shard, expert_shard)
    sums = lax.psum(jnp.concatenate(small_sums, 0), ("fsdp", "tp"))
    sums = lax.dynamic_slice_in_dim(sums, fsdp_index * shard, shard, 1)
    sums = sums.reshape(LAYERS, 2 + experts, shard)
    attn_grads = jnp.stack([grads[0] for grads in layer_grads]).astype(F32)
    expert_grads = jnp.stack([grads[1] for grads in layer_grads]).astype(F32)
    expert_grads = expert_grads.reshape(LAYERS, shard, experts, 2, hidden_units)
    qkv_grads = attn_grads[:, :, : 3 * heads_dim].reshape(LAYERS, shard, 3, heads_dim)
    return (
        hidden,
        upstream,
        jnp.transpose(qkv_grads, (0, 2, 1, 3)),
        jnp.transpose(attn_grads[:, :, 3 * heads_dim :], (0, 2, 1)),
        sums[:, 0],
        sums[:, 1],
        jnp.transpose(sums[:, 2:], (0, 2, 1)),
        jnp.transpose(expert_grads[:, :, :, 0], (0, 2, 1, 3)),
        jnp.transpose(expert_grads[:, :, :, 1], (0, 2, 3, 1)),
    )


def solution(mesh):
    return jax.shard_map(
        local,
        mesh=mesh,
        in_specs=(
            P(("fsdp", "tp"), None),
            P(("fsdp", "tp"), None),
            P(None, None, "fsdp", "tp"),
            P(None, "tp", "fsdp"),
            P(None, "fsdp"),
            P(None, "fsdp"),
            P(None, "fsdp", None),
            P(None, None, "fsdp", "tp"),
            P(None, None, "tp", "fsdp"),
            P("fsdp"),
            P("fsdp"),
        ),
        out_specs=(
            P(("fsdp", "tp"), None),
            P(("fsdp", "tp"), None),
            P(None, None, "fsdp", "tp"),
            P(None, "tp", "fsdp"),
            P(None, "fsdp"),
            P(None, "fsdp"),
            P(None, "fsdp", None),
            P(None, None, "fsdp", "tp"),
            P(None, None, "tp", "fsdp"),
        ),
        check_vma=False,
    )
```
